32 devices in a mesh: ops: 2 (over x), sec: 16 (over z, y, core).
Axes of the slice: x: 2, y: 2, z: 4, core: 2. Of those that a mesh axis runs over, the one named last changes fastest.
Arguments:
- wavefunction: float32 [128, 2, 128, 128], P('sec'), may hold values from -6 to 6
- left_blocks: float32 [16, 128, 128, 128], P('ops', 'sec'), may hold values from -0.5 to 0.5
- right_blocks: float32 [16, 128, 128, 128], P('ops', 'sec'), may hold values from -0.125 to 0.125
- target_owner: int32 [2, 16, 8, 8, 1], P('ops'), may hold values from 0 to 15; in each aligned block of 64 rows (0 to 63, 64 to 127, ..., all dimensions but the last counted through in order) at most 5 rows name the same one
- target_local: int32 [2, 16, 8, 8], P('ops'), may hold values from 0 to 7
Outputs:
- sigma: float32 [128, 2, 128, 128], P('sec', None, 'ops')
The draws below stay inside these ranges and needn't reach their ends.
Inputs may be any that keep to these rules, and one draw needn't show every extreme that they name: `target_owner`: among the 64 pairs [o, d, :, :, 0] of one device, at most 5 name the same owner, and some device's pairs name one owner exactly 5 times.
All inputs are finite; a program needn't handle non-finite values.
Results may differ from the reference program's by a relative error of at most 0.00013.
Values sent between devices are 32-bit elements; how exact they have to be, the bound alone decides.
No kernel may reach another device: no remote copies, remote signals or barrier semaphores. Data moves between devices by JAX's collectives and lax.ppermute only.
A program may use at most 192 MiB of HBM per device.

```python
import math
import jax
import jax.numpy as jnp
import numpy as np
from jax import lax

M = 128
NVEC = 2
TERM_DEV = 8
SEC_DEV = 8
TERMS = 16
NSEC = 128
CAP = 5
N_OPS = 2
N_SEC = 16


def place_ends(result, rng, low, largest):
    index_at = [jax.random.randint(jax.random.fold_in(rng, axis), (), 0, length) for axis, length in enumerate(result.shape)]
    main_axis = result.shape.index(max(result.shape))
    next_to = index_at[:main_axis] + [(index_at[main_axis] + 1) % result.shape[main_axis]] + index_at[main_axis + 1:]
    return result.at[tuple(index_at)].set(low).at[tuple(next_to)].set(largest)


def steps_of(key, shape, split, least, top_value):
    def one(position, shards_of):
        draws = jax.random.uniform(jax.random.fold_in(jax.random.fold_in(key, 6), position), (shards_of,), jnp.float32, least / len(split), top_value / len(split))
        return jnp.repeat(jnp.exp(draws), shape[position] // shards_of).reshape((-1,) + (1,) * (len(shape) - position - 1))

    factor_of = one(*split[0])
    for cut in split[1:]:
        factor_of = factor_of * one(*cut)
    return factor_of


def assign_block(key, own, number, rows, count, top, reach, lean):
    order = jax.random.permutation(key, count)
    heavy_load, common = shares(count, rows * top, reach, lean, True), shares(count, rows * top, reach, lean, False)
    places = jnp.arange(count)

    def named(tallies, rotation):
        used = int((tallies > 0).sum())
        fixed = max(1, used // 4)
        moved = fixed + (places - fixed + rotation * (used - fixed)) % max(1, count - fixed)
        return jnp.zeros((count,), jnp.int32).at[order[jnp.where(places < fixed, places, moved)]].set(jnp.asarray(tallies, jnp.int32))

    tallies = jnp.where(number % 4 == 0, named(heavy_load, number // 4), named(common, number - number // 4 - 1))
    mixed = jax.random.permutation(jax.random.fold_in(own, 3), count)
    source_of, sink = mixed[0:count // 2 * 2:2], mixed[1:count // 2 * 2:2]
    slack = jnp.minimum(tallies[source_of] - 1, reach - tallies[sink]) // 2
    slack = jnp.where((source_of == order[0]) | (sink == order[0]) | (tallies[sink] == 0), 0, jnp.maximum(slack, 0))
    moved = jax.random.randint(jax.random.fold_in(own, 4), (count // 2,), 0, 1 << 20) % (slack + 1)
    tallies = tallies.at[source_of].add(-moved).at[sink].add(moved)
    members = jnp.searchsorted(jnp.cumsum(tallies), jnp.arange(rows * top), side="right").astype(jnp.int32)
    table = members.reshape(top, rows).T
    table = table[jax.random.permutation(jax.random.fold_in(own, 1), rows)]
    rotation = jax.random.randint(jax.random.fold_in(own, 2), (rows, 1), 0, top)
    return jnp.take_along_axis(table, (jnp.arange(top)[None, :] + rotation) % top, axis=1)


def shares(amount, total, most, lean, full):
    portions = [(1 << 20) // math.isqrt(standing ** lean) + 1 for standing in range(1, amount + 1)]
    largest = most if full else min(most, max(-(-total // amount), total * portions[0] // sum(portions)))
    least = 1 if total - largest >= amount - 1 else 0
    given, surplus = [largest] + [least] * (amount - 1), total - largest - least * (amount - 1)
    while surplus > 0:
        free = [i for i in range(1, amount) if given[i] < largest] or [i for i in range(1, amount) if given[i] < most]
        pool, budget = sum([portions[i] for i in free]), surplus
        for i in free:
            addition = min(most - given[i], max(1, budget * portions[i] // pool), surplus)
            given[i] = given[i] + addition
            surplus = surplus - addition
    return np.array(given)


def centred(key, extent, width, reach, shards=(), kind=jnp.bfloat16):
    level = steps_of(key, extent, shards, -0.22, 0.18) if shards else 1.0
    entries = jax.random.normal(key, extent, jnp.float32) * width * level
    return jnp.minimum(jnp.maximum(entries, -reach), reach).astype(kind)


def setup_inputs(seed: int = 0) -> dict:
    keys = jax.random.split(jax.random.key(seed), 6)
    wavefunction = centred(keys[0], (NSEC, NVEC, M, M), 1.0, 6.0, ((0, 16),), jnp.float32)
    left_blocks = centred(keys[1], (TERMS, NSEC, M, M), M ** -0.5, 0.5, ((0, 2), (1, 16)), jnp.float32)
    right_blocks = centred(keys[2], (TERMS, NSEC, M, M), (M * TERMS) ** -0.5, 0.125, ((0, 2), (1, 16)), jnp.float32)
    target_owner_keys = jax.random.split(jax.random.fold_in(keys[3], 1), N_OPS * N_SEC * TERM_DEV * SEC_DEV // (TERM_DEV * SEC_DEV))
    target_owner_turns = jax.random.permutation(jax.random.fold_in(keys[3], 3), N_OPS * N_SEC * TERM_DEV * SEC_DEV // (TERM_DEV * SEC_DEV))
    target_owner = jax.vmap(lambda own, number: assign_block(jax.random.fold_in(keys[3], 2), own, number, TERM_DEV * SEC_DEV, N_SEC, 1, CAP, 2))(target_owner_keys, target_owner_turns).reshape((N_OPS, N_SEC, TERM_DEV, SEC_DEV, 1))
    target_local = place_ends(jax.random.randint(keys[4], (N_OPS, N_SEC, TERM_DEV, SEC_DEV), 0, SEC_DEV), jax.random.fold_in(keys[4], 1), 0, SEC_DEV - 1).astype(jnp.int32)
    return {"wavefunction": wavefunction, "left_blocks": left_blocks, "right_blocks": right_blocks, "target_owner": target_owner, "target_local": target_local}


def reference(wavefunction, left_blocks, right_blocks, target_owner, target_local):
    owner_table = jnp.transpose(target_owner[..., 0], (0, 2, 1, 3)).reshape(TERMS, NSEC)
    local_table = jnp.transpose(target_local, (0, 2, 1, 3)).reshape(TERMS, NSEC)
    targets = (owner_table * SEC_DEV + local_table).astype(jnp.int32)
    exact_mode = lax.Precision.HIGHEST

    def add_term(running, per_term):
        left_block, right_block, term_targets = per_term
        half_applied = jnp.einsum('svbe,sde->svbd', wavefunction.astype(jnp.float32), right_block.astype(jnp.float32), precision=exact_mode)
        contrib = jnp.einsum('sab,svbd->svad', left_block.astype(jnp.float32), half_applied, precision=exact_mode)
        return running + jax.ops.segment_sum(contrib, term_targets, num_segments=NSEC), None

    initial = jnp.zeros((NSEC, NVEC, M, M), jnp.float32)
    sigma, unused = lax.scan(add_term, initial, (left_blocks, right_blocks, targets))
    return sigma
```

```python
import functools

import jax
import jax.numpy as jnp
from jax import lax
from jax.experimental import pallas as pl
from jax.experimental.pallas import tpu as pltpu
from jax.sharding import PartitionSpec as P

CORES = 2
PLANES = 2
GROUP = 4


def coords(sec_count):
    me = lax.axis_index("sec")
    return me, me // (PLANES * CORES), (me // CORES) % PLANES, me % CORES


def find(code, sector_local, depth, z, y, rels):
    owner = code // sector_local
    local = code % sector_local
    core = owner % CORES
    y_rel = ((owner // CORES) % PLANES - y + PLANES) % PLANES
    z_rel = (owner // (CORES * PLANES) - z + depth) % depth
    inside = z_rel == rels[0]
    place = jnp.int32(0)
    for i, r in enumerate(rels[1:], 1):
        inside = inside | (z_rel == r)
        place = place + jnp.where(z_rel == r, i, 0)
    return inside, core, (place * PLANES + y_rel) * sector_local + local


def split(x):
    hi = x.astype(jnp.bfloat16)
    lo = (x - hi.astype(jnp.float32)).astype(jnp.bfloat16)
    return hi, lo


def apply_pair(left, right, psi_pair):
    m = left.shape[0]
    right_hi, right_lo = split(right)
    stacked = jnp.concatenate([right_hi, right_lo], axis=0)
    stacked = jnp.concatenate([stacked, stacked], axis=1)
    both = lax.dot_general(
        psi_pair, stacked, (((1,), (1,)), ((), ())), preferred_element_type=jnp.float32
    )
    half = both[:, :m] + both[:, m:]
    vectors = half.shape[0] // m
    half = jnp.concatenate([half[v * m : (v + 1) * m] for v in range(vectors)], axis=1)
    half_hi, half_lo = split(half)
    left_hi, left_lo = split(left)
    left_pair = jnp.concatenate([left_hi, left_lo], axis=1)
    out = jnp.dot(
        left_pair,
        jnp.concatenate([half_hi, half_hi], axis=0),
        preferred_element_type=jnp.float32,
    )
    return out + jnp.dot(left_hi, half_lo, preferred_element_type=jnp.float32)


def prepare(psi, psi_raw, psi_pairs, psi_sem):
    copy = pltpu.make_async_copy(psi, psi_raw, psi_sem)
    copy.wait()
    sectors, vectors, m, _ = psi_raw.shape

    def one(j, carry):
        hi, lo = split(psi_raw[j].reshape(vectors * m, m))
        psi_pairs[j] = jnp.concatenate([hi, lo], axis=1)
        return carry

    lax.fori_loop(0, sectors, one, 0)


def fetch(left, right, left_buf, right_buf, sems, pair, i, sectors):
    k, j = pair // sectors, pair % sectors
    return (
        pltpu.make_async_copy(left.at[k, j], left_buf.at[i], sems.at[i, 0]),
        pltpu.make_async_copy(right.at[k, j], right_buf.at[i], sems.at[i, 1]),
    )


def collect(table, base, pairs, wanted, note, begin):
    def one(p, count):
        hit, row = wanted(table[base + p])

        @pl.when(hit)
        def _():
            note(count, p, row)
            begin(count, p)

        return count + hit.astype(jnp.int32)

    return lax.fori_loop(0, pairs, one, jnp.int32(0))


def padded(count, note, begin, row):
    groups = (count + GROUP - 1) // GROUP
    for q in range(GROUP - 1):

        @pl.when(count + q < groups * GROUP)
        def _():
            note(count + q, 0, row)
            begin(count + q, 0)

    return groups


def group_products(g, listed, left, right, left_buf, right_buf, sems, psi_pairs, sectors):
    at = [g * GROUP + u for u in range(GROUP)]
    for i in at:
        for copy in fetch(left, right, left_buf, right_buf, sems, listed[i], i, sectors):
            copy.wait()
    return at, [
        apply_pair(left_buf[i], right_buf[i], psi_pairs[listed[i] % sectors]) for i in at
    ]


def sibling_kernel(
    rels, depth, table, psi, left, right, out,
    listed, left_buf, right_buf, psi_raw, psi_pairs, results, sems, psi_sem, out_sem,
):
    terms, sectors, m, _ = left.shape
    pairs = terms * sectors
    me, z, y, c = coords(None)
    pltpu.make_async_copy(psi, psi_raw, psi_sem).start()

    def wanted(code):
        inside, core, row = find(code, sectors, depth, z, y, rels)
        return inside & (core != c), row

    def note(i, p, row):
        listed[i] = p

    def begin(i, p):
        for copy in fetch(left, right, left_buf, right_buf, sems, p, i, sectors):
            copy.start()

    count = collect(table, me * pairs, pairs, wanted, note, begin)
    groups = padded(count, note, begin, 0)
    prepare(psi, psi_raw, psi_pairs, psi_sem)
    vectors = psi_raw.shape[1]

    def one(g, carry):
        at, products = group_products(
            g, listed, left, right, left_buf, right_buf, sems, psi_pairs, sectors
        )
        for i, product in zip(at, products):
            for v in range(vectors):
                results[i, v] = product[:, v * m : (v + 1) * m]
        for i in at:

            @pl.when(i < count)
            def _():
                pltpu.make_async_copy(results.at[i], out.at[i], out_sem.at[i]).start()

        return carry

    lax.fori_loop(0, groups, one, 0)

    def finish(i, carry):
        pltpu.make_async_copy(results.at[i], out.at[i], out_sem.at[i]).wait()
        return carry

    lax.fori_loop(0, count, finish, 0)


def dense_kernel(rels, depth, x_count, table, psi, left, right, arrived, *refs):
    terms, sectors, m, _ = left.shape
    vectors = psi.shape[1]
    pairs = terms * sectors
    planes = len(rels)
    out_count = x_count + PLANES + 2 * planes
    outs, refs = refs[:out_count], refs[out_count:]
    (
        listed, rows, rows_in, left_buf, right_buf, psi_raw, psi_pairs, arrivals, total,
        sems, psi_sem, in_sem, out_sems,
    ) = refs
    me, z, y, c = coords(None)
    x = lax.axis_index("ops")
    pltpu.make_async_copy(psi, psi_raw, psi_sem).start()
    pltpu.make_async_copy(arrived, arrivals, in_sem).start()
    target_count = total.shape[0] - 1

    def wanted(code):
        inside, core, row = find(code, sectors, depth, z, y, rels)
        return inside & (core == c), row

    def note(i, p, row):
        listed[i] = p
        rows[i] = row

    def begin(i, p):
        for copy in fetch(left, right, left_buf, right_buf, sems, p, i, sectors):
            copy.start()

    def note_in(i, p, row):
        rows_in[i] = row

    count = collect(table, me * pairs, pairs, wanted, note, begin)
    groups = padded(count, note, begin, target_count)
    sibling = me + 1 - 2 * c
    count_in = collect(table, sibling * pairs, pairs, wanted, note_in, lambda i, p: None)

    def clear(t, carry):
        total[t] = jnp.zeros(total.shape[1:], jnp.float32)
        return carry

    lax.fori_loop(0, target_count + 1, clear, 0)
    prepare(psi, psi_raw, psi_pairs, psi_sem)

    def one(g, carry):
        at, products = group_products(
            g, listed, left, right, left_buf, right_buf, sems, psi_pairs, sectors
        )
        for i, product in zip(at, products):
            row = rows[i]
            for v in range(vectors):
                total[row, v] += product[:, v * m : (v + 1) * m]
        return carry

    lax.fori_loop(0, groups, one, 0)
    pltpu.make_async_copy(arrived, arrivals, in_sem).wait()

    def merge(i, carry):
        total[rows_in[i]] += arrivals[i]
        return carry

    lax.fori_loop(0, count_in, merge, 0)

    first, second = pl.ds(0, sectors // 2), pl.ds(sectors // 2, sectors - sectors // 2)
    height = m // x_count
    copies = []

    def send(piece, iz, iy, which, v, x_rel):
        start = pl.multiple_of(((x + x_rel) % x_count) * height, 8)
        base = (iz * PLANES + iy) * sectors
        local = pl.ds(base + which.start, which.size)
        copies.append(
            pltpu.make_async_copy(
                total.at[local, v, pl.ds(start, height), :], piece, out_sems.at[len(copies)]
            )
        )

    for r in range(x_count):
        for iy in range(PLANES):
            for iz in range(planes):
                send(outs[r].at[iy, iz], iz, iy, first, 0, r)
    for iy in range(PLANES):
        for r in range(x_count):
            for iz in range(planes):
                send(outs[x_count + iy].at[r, iz], iz, iy, second, 0, r)
    for iz in range(planes):
        for r in range(x_count):
            for iy in range(PLANES):
                send(outs[x_count + PLANES + iz].at[r, iy], iz, iy, first, 1, r)
                send(outs[x_count + PLANES + planes + iz].at[iy, r], iz, iy, second, 1, r)
    for copy in copies:
        copy.start()
    for copy in copies:
        copy.wait()


def run_sibling(rels, depth, capacity, table, psi, left, right):
    terms, sectors, m, _ = left.shape
    vectors = psi.shape[1]
    slots = len(rels) * PLANES * capacity
    room = slots + GROUP - 1
    return pl.pallas_call(
        functools.partial(sibling_kernel, rels, depth),
        out_shape=jax.ShapeDtypeStruct((slots, vectors, m, m), jnp.float32),
        in_specs=[pl.BlockSpec(memory_space=pltpu.SMEM)] + [pl.BlockSpec(memory_space=pl.ANY)] * 3,
        out_specs=pl.BlockSpec(memory_space=pl.ANY),
        scratch_shapes=[
            pltpu.SMEM((room,), jnp.int32),
            pltpu.VMEM((room, m, m), jnp.float32),
            pltpu.VMEM((room, m, m), jnp.float32),
            pltpu.VMEM((sectors, vectors, m, m), jnp.float32),
            pltpu.VMEM((sectors, vectors * m, 2 * m), jnp.bfloat16),
            pltpu.VMEM((room, vectors, m, m), jnp.float32),
            pltpu.SemaphoreType.DMA((room, 2)),
            pltpu.SemaphoreType.DMA,
            pltpu.SemaphoreType.DMA((room,)),
        ],
        compiler_params=pltpu.CompilerParams(vmem_limit_bytes=48 << 20),
        name="sibling_contributions",
    )(table, psi, left, right)


def run_dense(rels, depth, capacity, x_count, table, psi, left, right, arrived):
    terms, sectors, m, _ = left.shape
    vectors = psi.shape[1]
    planes = len(rels)
    slots = planes * PLANES * capacity
    room = slots + GROUP - 1
    targets = planes * PLANES * sectors
    half, height = sectors // 2, m // x_count
    shapes = (
        [(PLANES, planes, half, height, m)] * x_count
        + [(x_count, planes, half, height, m)] * PLANES
        + [(x_count, PLANES, half, height, m)] * planes
        + [(PLANES, x_count, half, height, m)] * planes
    )
    pieces = 4 * x_count * PLANES * planes
    return pl.pallas_call(
        functools.partial(dense_kernel, rels, depth, x_count),
        out_shape=[jax.ShapeDtypeStruct(s, jnp.float32) for s in shapes],
        in_specs=[pl.BlockSpec(memory_space=pltpu.SMEM)] + [pl.BlockSpec(memory_space=pl.ANY)] * 4,
        out_specs=[pl.BlockSpec(memory_space=pl.ANY)] * len(shapes),
        scratch_shapes=[
            pltpu.SMEM((room,), jnp.int32),
            pltpu.SMEM((room,), jnp.int32),
            pltpu.SMEM((room,), jnp.int32),
            pltpu.VMEM((room, m, m), jnp.float32),
            pltpu.VMEM((room, m, m), jnp.float32),
            pltpu.VMEM((sectors, vectors, m, m), jnp.float32),
            pltpu.VMEM((sectors, vectors * m, 2 * m), jnp.bfloat16),
            pltpu.VMEM((slots, vectors, m, m), jnp.float32),
            pltpu.VMEM((targets + 1, vectors, m, m), jnp.float32),
            pltpu.SemaphoreType.DMA((room, 2)),
            pltpu.SemaphoreType.DMA,
            pltpu.SemaphoreType.DMA,
            pltpu.SemaphoreType.DMA((pieces,)),
        ],
        compiler_params=pltpu.CompilerParams(vmem_limit_bytes=56 << 20),
        name="dense_sums",
    )(table, psi, left, right, arrived)


def shards(wavefunction, left_blocks, right_blocks, target_owner, target_local):
    sec_count = lax.axis_size("sec")
    x_count = lax.axis_size("ops")
    depth = sec_count // (PLANES * CORES)
    terms, sectors = left_blocks.shape[:2]
    pairs = terms * sectors
    capacity = (pairs + sec_count - 1) // sec_count + 1
    table = (target_owner[0, :, :, :, 0] * sectors + target_local[0]).reshape(sec_count * pairs)

    def at(z, y, c):
        return ((z % depth) * PLANES + y % PLANES) * CORES + c % CORES

    everyone = [(z, y, c) for z in range(depth) for y in range(PLANES) for c in range(CORES)]
    swap_core = [(at(z, y, c), at(z, y, c + 1)) for z, y, c in everyone]
    next_y = [(at(z, y, c), at(z, y + 1, c)) for z, y, c in everyone]
    up = [(at(z, y, c), at(z + 1, y, c)) for z, y, c in everyone]
    down = [(at(z, y, c), at(z - 1, y, c)) for z, y, c in everyone]
    next_x = [(i, (i + 1) % x_count) for i in range(x_count)]

    def ring(parts, axis, steps):
        moving = parts[0]
        for part in parts[1:]:
            moving = lax.ppermute(moving, axis, steps) + part
        return moving

    def over_x(parts):
        return ring([parts[r] for r in range(x_count - 1, -1, -1)], "ops", next_x)

    def over_y(parts):
        return ring([parts[r] for r in range(PLANES - 1, -1, -1)], "sec", next_y)

    def over_z_up(parts):
        return ring([parts[r] for r in range(depth - 1, -1, -1)], "sec", up)

    def over_z_down(parts):
        return ring([parts[r] for r in [*range(1, depth), 0]], "sec", down)

    near = sorted({1 % depth, (depth - 1) % depth} - {0})
    chunks = [c for c in (near, [r for r in range(depth) if r not in near]) if c]
    moved = [
        lax.ppermute(
            run_sibling(rels, depth, capacity, table, wavefunction, left_blocks, right_blocks),
            "sec",
            swap_core,
        )
        for rels in chunks
    ]
    first_a, second_a, first_b, second_b = {}, {}, {}, {}
    for rels, arrived in zip(chunks, moved):
        sums = run_dense(
            rels, depth, capacity, x_count, table, wavefunction, left_blocks, right_blocks, arrived
        )
        planes = len(rels)
        by_x, by_y = sums[:x_count], sums[x_count : x_count + PLANES]
        rest = sums[x_count + PLANES :]
        a1, a2 = over_y(over_x(by_x)), over_x(over_y(by_y))
        for i, r in enumerate(rels):
            first_a[r], second_a[r] = a1[i], a2[i]
            first_b[r], second_b[r] = rest[i], rest[planes + i]
    b1 = over_y(over_x(over_z_up(first_b)))
    b2 = over_x(over_y(over_z_down(second_b)))
    a1, a2 = over_z_up(first_a), over_z_down(second_a)
    return jnp.stack([jnp.concatenate([a1, a2], 0), jnp.concatenate([b1, b2], 0)], axis=1)


def solution(mesh):
    placed = (
        P("sec", None, None, None),
        P("ops", "sec", None, None),
        P("ops", "sec", None, None),
        P("ops", None, None, None, None),
        P("ops", None, None, None),
    )
    return jax.shard_map(
        shards, mesh=mesh, in_specs=placed, out_specs=P("sec", None, "ops", None), check_vma=False
    )
```

```python
import functools

import jax
import jax.numpy as jnp
from jax import lax
from jax.experimental import pallas as pl
from jax.experimental.pallas import tpu as pltpu
from jax.sharding import PartitionSpec as P

CORES = 2
PLANES = 2
MOST_IN_GROUP = 10


def split(x):
    hi = x.astype(jnp.bfloat16)
    lo = (x - hi.astype(jnp.float32)).astype(jnp.bfloat16)
    return hi, lo


def apply_pair(left, right, psi_pair):
    m = left.shape[0]
    right_hi, right_lo = split(right)
    stacked = jnp.concatenate([right_hi, right_lo], axis=0)
    stacked = jnp.concatenate([stacked, stacked], axis=1)
    both = lax.dot_general(
        psi_pair, stacked, (((1,), (1,)), ((), ())), preferred_element_type=jnp.float32
    )
    half = both[:, :m] + both[:, m:]
    vectors = half.shape[0] // m
    half = jnp.concatenate([half[v * m : (v + 1) * m] for v in range(vectors)], axis=1)
    half_hi, half_lo = split(half)
    left_hi, left_lo = split(left)
    left_pair = jnp.concatenate([left_hi, left_lo], axis=1)
    out = jnp.dot(
        left_pair,
        jnp.concatenate([half_hi, half_hi], axis=0),
        preferred_element_type=jnp.float32,
    )
    return out + jnp.dot(left_hi, half_lo, preferred_element_type=jnp.float32)


def prepare(psi, psi_raw, psi_pairs, psi_sem):
    pltpu.make_async_copy(psi, psi_raw, psi_sem).wait()
    sectors, vectors, m, _ = psi_raw.shape

    def one(j, carry):
        hi, lo = split(psi_raw[j].reshape(vectors * m, m))
        psi_pairs[j] = jnp.concatenate([hi, lo], axis=1)
        return carry

    lax.fori_loop(0, sectors, one, 0)


def fetch(left, right, left_buf, right_buf, sems, pair, i, sectors):
    k, j = pair // sectors, pair % sectors
    return (
        pltpu.make_async_copy(left.at[k, j], left_buf.at[i], sems.at[i, 0]),
        pltpu.make_async_copy(right.at[k, j], right_buf.at[i], sems.at[i, 1]),
    )


def collect(codes, base, pairs, low, size, take):
    def one(p, count):
        row = codes[base + p] - low
        hit = (row >= 0) & (row < size)

        @pl.when(hit)
        def _():
            take(count, p, row)

        return count + hit.astype(jnp.int32)

    return lax.fori_loop(0, pairs, one, jnp.int32(0), unroll=4)


def padded(count, group, take, row):
    groups = (count + group - 1) // group

    def one(i, carry):
        take(i, 0, row)
        return carry

    lax.fori_loop(count, groups * group, one, 0)
    return groups


def group_products(g, group, listed, left, right, left_buf, right_buf, sems, psi_pairs, sectors):
    at = [g * group + u for u in range(group)]
    for i in at:
        for copy in fetch(left, right, left_buf, right_buf, sems, listed[i], i, sectors):
            copy.wait()
    return at, [
        apply_pair(left_buf[i], right_buf[i], psi_pairs[listed[i] % sectors]) for i in at
    ]


def sibling_kernel(
    low, size, group, codes, psi, left, right, out,
    listed, left_buf, right_buf, psi_raw, psi_pairs, sems, psi_sem,
):
    terms, sectors, m, _ = left.shape
    vectors = psi.shape[1]
    pltpu.make_async_copy(psi, psi_raw, psi_sem).start()

    def take(i, p, row):
        listed[i] = p
        for copy in fetch(left, right, left_buf, right_buf, sems, p, i, sectors):
            copy.start()

    count = collect(codes, 0, terms * sectors, low, size, take)
    groups = padded(count, group, take, 0)
    prepare(psi, psi_raw, psi_pairs, psi_sem)

    def one(g, carry):
        at, products = group_products(
            g, group, listed, left, right, left_buf, right_buf, sems, psi_pairs, sectors
        )
        for i, product in zip(at, products):
            for v in range(vectors):
                out[i, v] = product[:, v * m : (v + 1) * m]
        return carry

    lax.fori_loop(0, groups, one, 0)


def dense_kernel(
    low, size, group, x_count, codes, psi, left, right, arrived, total,
    listed, rows, rows_in, left_buf, right_buf, psi_raw, psi_pairs, sems, psi_sem,
):
    terms, sectors, m, _ = left.shape
    vectors = psi.shape[1]
    pairs = terms * sectors
    height = m // x_count
    x, core = lax.axis_index("ops"), lax.axis_index("sec") % CORES
    pltpu.make_async_copy(psi, psi_raw, psi_sem).start()

    def take(i, p, row):
        listed[i] = p
        rows[i] = row
        for copy in fetch(left, right, left_buf, right_buf, sems, p, i, sectors):
            copy.start()

    def take_in(i, p, row):
        rows_in[i] = row

    count = collect(codes, 0, pairs, low, size, take)
    groups = padded(count, group, take, size)
    count_in = collect(codes, pairs, pairs, low, size, take_in)

    def clear(t, carry):
        total[t] = jnp.zeros(total.shape[1:], jnp.float32)
        return carry

    lax.fori_loop(0, size // PLANES + 1, clear, 0)
    prepare(psi, psi_raw, psi_pairs, psi_sem)

    def add(code, block):
        row, y_rel = code // PLANES, code % PLANES
        for h in range(x_count):
            x_rel = lax.rem(h - x + x_count, x_count)
            place = x_rel * PLANES + y_rel
            if x_count == PLANES:
                place = jnp.where(core == 0, place, y_rel * PLANES + x_rel)
            for v in range(vectors):
                total[row, v, place] += block(v, h * height)

    def one(g, carry):
        at, products = group_products(
            g, group, listed, left, right, left_buf, right_buf, sems, psi_pairs, sectors
        )
        for i, product in zip(at, products):
            add(rows[i], lambda v, h: product[h : h + height, v * m : (v + 1) * m])
        return carry

    lax.fori_loop(0, groups, one, 0)

    def merge(i, carry):
        add(rows_in[i], lambda v, h: arrived[i, v, h : h + height])
        return carry

    lax.fori_loop(0, count_in, merge, 0)


def group_of(slots):
    return max(d for d in range(1, MOST_IN_GROUP + 1) if slots % d == 0)


def buffers(slots, sectors, vectors, m):
    return [
        pltpu.VMEM((slots, m, m), jnp.float32),
        pltpu.VMEM((slots, m, m), jnp.float32),
        pltpu.VMEM((sectors, vectors, m, m), jnp.float32),
        pltpu.VMEM((sectors, vectors * m, 2 * m), jnp.bfloat16),
        pltpu.SemaphoreType.DMA((slots, 2)),
        pltpu.SemaphoreType.DMA,
    ]


def cost(slots, vectors, m):
    return pl.CostEstimate(
        flops=slots * vectors * 16 * m**3,
        bytes_accessed=slots * (2 + vectors) * m * m * 4,
        transcendentals=0,
    )


def in_hbm(*arrays):
    return [pltpu.with_memory_space_constraint(a, pltpu.HBM) for a in arrays]


def run_sibling(low, size, slots, codes, psi, left, right):
    sectors, m = left.shape[1], left.shape[2]
    vectors = psi.shape[1]
    return pl.pallas_call(
        functools.partial(sibling_kernel, low, size, group_of(slots)),
        out_shape=pltpu.VMEM((slots, vectors, m, m), jnp.float32),
        in_specs=[pl.BlockSpec(memory_space=pltpu.SMEM)] + [pl.BlockSpec(memory_space=pl.ANY)] * 3,
        out_specs=pl.BlockSpec(memory_space=pltpu.VMEM),
        scratch_shapes=[pltpu.SMEM((slots,), jnp.int32), *buffers(slots, sectors, vectors, m)],
        compiler_params=pltpu.CompilerParams(vmem_limit_bytes=24 << 20),
        cost_estimate=cost(slots, vectors, m),
        name="sibling_contributions",
    )(codes, *in_hbm(psi, left, right))


def run_dense(low, size, slots, x_count, codes, psi, left, right, arrived):
    sectors, m = left.shape[1], left.shape[2]
    vectors = psi.shape[1]
    shape = (size // PLANES + 1, vectors, x_count * PLANES, m // x_count, m)
    return pl.pallas_call(
        functools.partial(dense_kernel, low, size, group_of(slots), x_count),
        out_shape=pltpu.VMEM(shape, jnp.float32),
        in_specs=[pl.BlockSpec(memory_space=pltpu.SMEM)]
        + [pl.BlockSpec(memory_space=pl.ANY)] * 3
        + [pl.BlockSpec(memory_space=pltpu.VMEM)],
        out_specs=pl.BlockSpec(memory_space=pltpu.VMEM),
        scratch_shapes=[pltpu.SMEM((slots,), jnp.int32)] * 3
        + buffers(slots, sectors, vectors, m),
        compiler_params=pltpu.CompilerParams(vmem_limit_bytes=32 << 20),
        cost_estimate=cost(slots, vectors, m),
        name="dense_sums",
    )(codes, *in_hbm(psi, left, right), arrived)


def shards(wavefunction, left_blocks, right_blocks, target_owner, target_local):
    sec_count = lax.axis_size("sec")
    x_count = lax.axis_size("ops")
    depth = sec_count // (PLANES * CORES)
    terms, sectors, m, _ = left_blocks.shape
    pairs = terms * sectors
    capacity = (pairs + sec_count - 1) // sec_count + 1
    me = lax.axis_index("sec")
    z, y, c = me // (PLANES * CORES), (me // CORES) % PLANES, me % CORES

    chunks = [list(range(1, depth // 2 + 1)), [*range(depth // 2 + 1, depth), 0]]
    order = [r for chunk in chunks for r in chunk]

    def rows_of(table):
        return jnp.concatenate(
            [lax.dynamic_slice_in_dim(table, d, 1, 0) for d in (me, me + 1 - 2 * c)]
        ).reshape(2 * pairs)

    owner = rows_of(target_owner[0, :, :, :, 0].reshape(sec_count, pairs))
    local = rows_of(target_local[0].reshape(sec_count, pairs))
    z_rel = (owner // (CORES * PLANES) - z + depth) % depth
    z_place = sum(jnp.where(z_rel == r, i, 0) for i, r in enumerate(order))
    y_rel = ((owner // CORES) % PLANES - y + PLANES) % PLANES
    c_rel = (owner % CORES - c + CORES) % CORES
    codes = ((c_rel * depth + z_place) * sectors + local) * PLANES + y_rel

    def at(x, z, y, c):
        place = ((z % depth) * PLANES + y % PLANES) * CORES + c % CORES
        return x % x_count * sec_count + place

    everyone = [
        (x, z, y, c)
        for x in range(x_count)
        for z in range(depth)
        for y in range(PLANES)
        for c in range(CORES)
    ]

    def to(target):
        return [(at(*d), at(*target(*d))) for d in everyone]

    swap_core = to(lambda x, z, y, c: (x, z, y, c + 1))
    next_x = to(lambda x, z, y, c: (x + 1, z, y, c))
    next_y = to(lambda x, z, y, c: (x, z, y + 1, c))
    shift = [to(lambda x, z, y, c, r=r: (x, z + r, y, c)) for r in range(depth)]
    first, second = next_x, next_y
    if x_count == PLANES:
        first = to(lambda x, z, y, c: (x + 1, z, y, c) if c == 0 else (x, z, y + 1, c))
        second = to(lambda x, z, y, c: (x, z, y + 1, c) if c == 0 else (x + 1, z, y, c))

    def send(message, perm):
        return lax.ppermute(message, ("ops", "sec"), perm)

    def ring(parts, perm):
        moving = parts[-1]
        for part in parts[-2::-1]:
            moving = send(moving, perm) + part
        return moving

    def fold_first(sums):
        return ring([sums[:, :, p] for p in range(x_count)], first)

    def fold_second(sums):
        return ring([sums[:, :, q] for q in range(PLANES)], second)

    moved, spans = [], []
    start = 0
    for rels in chunks:
        size = len(rels) * PLANES * sectors
        slots = len(rels) * PLANES * capacity
        low = start * PLANES * sectors
        spans.append((low, size, slots))
        start += len(rels)
        sent = run_sibling(
            low + depth * PLANES * sectors, size, slots, codes,
            wavefunction, left_blocks, right_blocks,
        )
        moved.append(send(sent, swap_core))
    height, cut = m // x_count, sectors - sectors // 4
    early, late = {}, {}
    for rels, arrived, (low, size, slots) in zip(chunks, moved, spans):
        planes = len(rels)
        sums = run_dense(
            low, size, slots, x_count, codes, wavefunction, left_blocks, right_blocks, arrived
        )
        sums = sums[: planes * sectors].reshape(planes, sectors, -1, x_count, PLANES, height, m)
        for i, r in enumerate(rels):
            early[r] = sums[i, cut:, 1][None]
        folded = fold_second(
            fold_first(jnp.concatenate([sums[:, :, 0], sums[:, :cut, 1]], axis=1))
        )
        for i, r in enumerate(rels):
            late[r] = folded[i]
    by_z = [(send(early[r], shift[r]) if r else early[r]) for r in order]
    tail = fold_second(fold_first(sum(by_z[1:], by_z[0])))[0]
    by_z = [(send(late[r], shift[r]) if r else late[r]) for r in order]
    main = sum(by_z[1:], by_z[0])
    return jnp.stack([main[:sectors], jnp.concatenate([main[sectors:], tail])], axis=1)


def solution(mesh):
    placed = (
        P("sec", None, None, None),
        P("ops", "sec", None, None),
        P("ops", "sec", None, None),
        P("ops", None, None, None, None),
        P("ops", None, None, None),
    )
    return jax.shard_map(
        shards, mesh=mesh, in_specs=placed, out_specs=P("sec", None, "ops", None), check_vma=False
    )
```

```python
import functools

import jax
import jax.numpy as jnp
from jax import lax
from jax.experimental import pallas as pl
from jax.experimental.pallas import tpu as pltpu
from jax.sharding import PartitionSpec as P

CORES = 2
PLANES = 2
MOST_IN_GROUP = 10


def split(x):
    hi = x.astype(jnp.bfloat16)
    lo = (x - hi.astype(jnp.float32)).astype(jnp.bfloat16)
    return hi, lo


def apply_pair(left, right, psi_pair):
    m = left.shape[0]
    right_hi, right_lo = split(right)
    stacked = jnp.concatenate([right_hi, right_lo], axis=0)
    stacked = jnp.concatenate([stacked, stacked], axis=1)
    both = lax.dot_general(
        psi_pair, stacked, (((1,), (1,)), ((), ())), preferred_element_type=jnp.float32
    )
    half = both[:, :m] + both[:, m:]
    vectors = half.shape[0] // m
    half = jnp.concatenate([half[v * m : (v + 1) * m] for v in range(vectors)], axis=1)
    half_hi, half_lo = split(half)
    left_hi, left_lo = split(left)
    left_pair = jnp.concatenate([left_hi, left_lo], axis=1)
    out = jnp.dot(
        left_pair,
        jnp.concatenate([half_hi, half_hi], axis=0),
        preferred_element_type=jnp.float32,
    )
    return out + jnp.dot(left_hi, half_lo, preferred_element_type=jnp.float32)


def prepare(psi, psi_raw, psi_pairs, psi_sem):
    pltpu.make_async_copy(psi, psi_raw, psi_sem).wait()
    sectors, vectors, m, _ = psi_raw.shape

    def one(j, carry):
        hi, lo = split(psi_raw[j].reshape(vectors * m, m))
        psi_pairs[j] = jnp.concatenate([hi, lo], axis=1)
        return carry

    lax.fori_loop(0, sectors, one, 0)


def fetch(left, right, left_buf, right_buf, sems, pair, i, sectors):
    k, j = pair // sectors, pair % sectors
    return (
        pltpu.make_async_copy(left.at[k, j], left_buf.at[i], sems.at[i, 0]),
        pltpu.make_async_copy(right.at[k, j], right_buf.at[i], sems.at[i, 1]),
    )


def collect(codes, base, pairs, low, size, take):
    def one(p, count):
        row = codes[base + p] - low
        hit = (row >= 0) & (row < size)

        @pl.when(hit)
        def _():
            take(count, p, row)

        return count + hit.astype(jnp.int32)

    return lax.fori_loop(0, pairs, one, jnp.int32(0), unroll=4)


def padded(count, group, take, row):
    groups = (count + group - 1) // group

    def one(i, carry):
        take(i, 0, row)
        return carry

    lax.fori_loop(count, groups * group, one, 0)
    return groups


def group_products(g, group, listed, left, right, left_buf, right_buf, sems, psi_pairs, sectors):
    at = [g * group + u for u in range(group)]
    for i in at:
        for copy in fetch(left, right, left_buf, right_buf, sems, listed[i], i, sectors):
            copy.wait()
    return at, [
        apply_pair(left_buf[i], right_buf[i], psi_pairs[listed[i] % sectors]) for i in at
    ]


def sibling_kernel(
    low, size, group, codes, psi, left, right, out,
    listed, left_buf, right_buf, psi_raw, psi_pairs, sems, psi_sem,
):
    terms, sectors, m, _ = left.shape
    vectors = psi.shape[1]
    pltpu.make_async_copy(psi, psi_raw, psi_sem).start()

    def take(i, p, row):
        listed[i] = p
        for copy in fetch(left, right, left_buf, right_buf, sems, p, i, sectors):
            copy.start()

    count = collect(codes, 0, terms * sectors, low, size, take)
    groups = padded(count, group, take, 0)
    prepare(psi, psi_raw, psi_pairs, psi_sem)

    def one(g, carry):
        at, products = group_products(
            g, group, listed, left, right, left_buf, right_buf, sems, psi_pairs, sectors
        )
        for i, product in zip(at, products):
            for v in range(vectors):
                out[i, v] = product[:, v * m : (v + 1) * m]
        return carry

    lax.fori_loop(0, groups, one, 0)


def dense_kernel(
    low, size, group, x_count, codes, psi, left, right, arrived, total,
    listed, rows, rows_in, left_buf, right_buf, psi_raw, psi_pairs, sems, psi_sem,
):
    terms, sectors, m, _ = left.shape
    vectors = psi.shape[1]
    pairs = terms * sectors
    height = m // x_count
    x, core = lax.axis_index("ops"), lax.axis_index("sec") % CORES
    pltpu.make_async_copy(psi, psi_raw, psi_sem).start()

    def take(i, p, row):
        listed[i] = p
        rows[i] = row
        for copy in fetch(left, right, left_buf, right_buf, sems, p, i, sectors):
            copy.start()

    def take_in(i, p, row):
        rows_in[i] = row

    count = collect(codes, 0, pairs, low, size, take)
    groups = padded(count, group, take, size)
    count_in = collect(codes, pairs, pairs, low, size, take_in)

    def clear(t, carry):
        total[t // sectors, t % sectors] = jnp.zeros(total.shape[2:], jnp.float32)
        return carry

    lax.fori_loop(0, size // PLANES + 1, clear, 0)
    prepare(psi, psi_raw, psi_pairs, psi_sem)

    def add(code, block):
        row, y_rel = code // PLANES, code % PLANES
        plane, local = row // sectors, row % sectors
        for h in range(x_count):
            x_rel = lax.rem(h - x + x_count, x_count)
            place = x_rel * PLANES + y_rel
            if x_count == PLANES:
                place = jnp.where(core == 0, place, y_rel * PLANES + x_rel)
            for v in range(vectors):
                total[plane, local, v, place] += block(v, h * height)

    def one(g, carry):
        at, products = group_products(
            g, group, listed, left, right, left_buf, right_buf, sems, psi_pairs, sectors
        )
        for i, product in zip(at, products):
            add(rows[i], lambda v, h: product[h : h + height, v * m : (v + 1) * m])
        return carry

    lax.fori_loop(0, groups, one, 0)

    def merge(i, carry):
        add(rows_in[i], lambda v, h: arrived[i, v, h : h + height])
        return carry

    lax.fori_loop(0, count_in, merge, 0)


def group_of(slots):
    return max(d for d in range(1, MOST_IN_GROUP + 1) if slots % d == 0)


def buffers(slots, sectors, vectors, m):
    return [
        pltpu.VMEM((slots, m, m), jnp.float32),
        pltpu.VMEM((slots, m, m), jnp.float32),
        pltpu.VMEM((sectors, vectors, m, m), jnp.float32),
        pltpu.VMEM((sectors, vectors * m, 2 * m), jnp.bfloat16),
        pltpu.SemaphoreType.DMA((slots, 2)),
        pltpu.SemaphoreType.DMA,
    ]


def cost(slots, vectors, m):
    return pl.CostEstimate(
        flops=slots * vectors * 16 * m**3,
        bytes_accessed=slots * (2 + vectors) * m * m * 4,
        transcendentals=0,
    )


def in_hbm(*arrays):
    return [pltpu.with_memory_space_constraint(a, pltpu.HBM) for a in arrays]


def run_sibling(low, size, slots, codes, psi, left, right):
    sectors, m = left.shape[1], left.shape[2]
    vectors = psi.shape[1]
    return pl.pallas_call(
        functools.partial(sibling_kernel, low, size, group_of(slots)),
        out_shape=pltpu.VMEM((slots, vectors, m, m), jnp.float32),
        in_specs=[pl.BlockSpec(memory_space=pltpu.SMEM)] + [pl.BlockSpec(memory_space=pl.ANY)] * 3,
        out_specs=pl.BlockSpec(memory_space=pltpu.VMEM),
        scratch_shapes=[pltpu.SMEM((slots,), jnp.int32), *buffers(slots, sectors, vectors, m)],
        compiler_params=pltpu.CompilerParams(vmem_limit_bytes=24 << 20),
        cost_estimate=cost(slots, vectors, m),
        name="sibling_contributions",
    )(codes, *in_hbm(psi, left, right))


def run_dense(low, size, slots, x_count, codes, psi, left, right, arrived):
    sectors, m = left.shape[1], left.shape[2]
    vectors = psi.shape[1]
    planes = size // (PLANES * sectors)
    shape = (planes + 1, sectors, vectors, x_count * PLANES, m // x_count, m)
    return pl.pallas_call(
        functools.partial(dense_kernel, low, size, group_of(slots), x_count),
        out_shape=pltpu.VMEM(shape, jnp.float32),
        in_specs=[pl.BlockSpec(memory_space=pltpu.SMEM)]
        + [pl.BlockSpec(memory_space=pl.ANY)] * 3
        + [pl.BlockSpec(memory_space=pltpu.VMEM)],
        out_specs=pl.BlockSpec(memory_space=pltpu.VMEM),
        scratch_shapes=[pltpu.SMEM((slots,), jnp.int32)] * 3
        + buffers(slots, sectors, vectors, m),
        compiler_params=pltpu.CompilerParams(vmem_limit_bytes=32 << 20),
        cost_estimate=cost(slots, vectors, m),
        name="dense_sums",
    )(codes, *in_hbm(psi, left, right), arrived)


def shards(wavefunction, left_blocks, right_blocks, target_owner, target_local):
    sec_count = lax.axis_size("sec")
    x_count = lax.axis_size("ops")
    depth = sec_count // (PLANES * CORES)
    terms, sectors, m, _ = left_blocks.shape
    pairs = terms * sectors
    capacity = (pairs + sec_count - 1) // sec_count + 1
    me = lax.axis_index("sec")
    z, y, c = me // (PLANES * CORES), (me // CORES) % PLANES, me % CORES

    chunks = [list(range(depth // 2, 0, -1)), [*range(depth // 2 + 1, depth), 0]]
    order = [r for chunk in chunks for r in chunk]

    def rows_of(table):
        return jnp.concatenate(
            [lax.dynamic_slice_in_dim(table, d, 1, 0) for d in (me, me + 1 - 2 * c)]
        ).reshape(2 * pairs)

    owner = rows_of(target_owner[0, :, :, :, 0].reshape(sec_count, pairs))
    local = rows_of(target_local[0].reshape(sec_count, pairs))
    z_rel = (owner // (CORES * PLANES) - z + depth) % depth
    z_place = sum(jnp.where(z_rel == r, i, 0) for i, r in enumerate(order))
    y_rel = ((owner // CORES) % PLANES - y + PLANES) % PLANES
    c_rel = (owner % CORES - c + CORES) % CORES
    codes = ((c_rel * depth + z_place) * sectors + local) * PLANES + y_rel

    def at(x, z, y, c):
        place = ((z % depth) * PLANES + y % PLANES) * CORES + c % CORES
        return x % x_count * sec_count + place

    everyone = [
        (x, z, y, c)
        for x in range(x_count)
        for z in range(depth)
        for y in range(PLANES)
        for c in range(CORES)
    ]

    def to(target):
        return [(at(*d), at(*target(*d))) for d in everyone]

    swap_core = to(lambda x, z, y, c: (x, z, y, c + 1))
    next_x = to(lambda x, z, y, c: (x + 1, z, y, c))
    next_y = to(lambda x, z, y, c: (x, z, y + 1, c))
    shift = [to(lambda x, z, y, c, r=r: (x, z + r, y, c)) for r in range(depth)]
    first, second = next_x, next_y
    if x_count == PLANES:
        first = to(lambda x, z, y, c: (x + 1, z, y, c) if c == 0 else (x, z, y + 1, c))
        second = to(lambda x, z, y, c: (x, z, y + 1, c) if c == 0 else (x + 1, z, y, c))

    def send(message, perm):
        return lax.ppermute(message, ("ops", "sec"), perm)

    def ring(parts, perm, *done):
        moving = parts[-1]
        for part in parts[-2::-1]:
            moving = after(send(moving, perm), *done) + part
        return moving

    def fold_first(sums, *done):
        parts = [sums[:, p * PLANES : (p + 1) * PLANES] for p in range(x_count)]
        return ring(parts, first, *done)

    def fold_second(sums):
        return ring([sums[:, q] for q in range(PLANES)], second)

    def after(value, *done):
        return lax.optimization_barrier((value, done))[0]

    arrays = (wavefunction, left_blocks, right_blocks)
    spans, sent = [], []
    start = 0
    for rels in chunks:
        span = [PLANES * n for n in (start * sectors, len(rels) * sectors, len(rels) * capacity)]
        spans.append(span)
        sent.append(run_sibling(span[0] + depth * PLANES * sectors, *span[1:], codes, *arrays))
        start += len(rels)
    sums, arrived, by_rel = [], [], {}
    for rels, span, message in zip(chunks, spans, sent):
        arrived.append(send(after(message, *sums[-1:]), swap_core))
        sums.append(run_dense(*span, x_count, codes, *arrays, arrived[-1]))
        for i, r in enumerate(rels):
            by_rel[r] = sums[-1][i]

    cut = sectors // 2
    early = {
        r: send(after(by_rel[r][cut:, 1], arrived[-1]), shift[r]) for r in (1, depth - 1)
    }

    def piece_of(r):
        count = cut if r == 0 or r in early else sectors
        return jnp.concatenate([by_rel[r][:, 0], by_rel[r][:count, 1]])

    halves, late = [], []
    for i, r in enumerate(order):
        piece = piece_of(r)
        if i == 1:
            piece = after(piece, arrived[-1])
        if i > 1:
            piece = after(piece, halves[i - 2])
        done = [sums[-1]] if i == 0 else [whole] if i == 1 else []
        halves.append(fold_first(piece, *done))
        whole = fold_second(halves[i])
        late.append(send(whole, shift[r]) if r else whole)
    tail = after(by_rel[0][cut:, 1] + sum(early.values()), halves[-1])
    tail = fold_second(after(fold_first(tail), late[0]))
    common = sectors + cut
    total = sum(w[:common] for w in late)
    tail = tail + sum(w[common:] for w in late if w.shape[0] > common)
    return jnp.stack([total[:sectors], jnp.concatenate([total[sectors:], tail])], axis=1)


def solution(mesh):
    placed = (
        P("sec", None, None, None),
        P("ops", "sec", None, None),
        P("ops", "sec", None, None),
        P("ops", None, None, None, None),
        P("ops", None, None, None),
    )
    return jax.shard_map(
        shards, mesh=mesh, in_specs=placed, out_specs=P("sec", None, "ops", None), check_vma=False
    )
```

```python
import functools

import jax
import jax.numpy as jnp
from jax import lax
from jax.experimental import pallas as pl
from jax.experimental.pallas import tpu as pltpu
from jax.sharding import PartitionSpec as P

CORES = 2
PLANES = 2
VECTORS = 2
MOST_IN_GROUP = 10


def split(x):
    hi = x.astype(jnp.bfloat16)
    lo = (x - hi.astype(jnp.float32)).astype(jnp.bfloat16)
    return hi, lo


def apply_pair(left, right, psi_pair):
    m = left.shape[0]
    right_hi, right_lo = split(right)
    stacked = jnp.concatenate([right_hi, right_lo], axis=0)
    stacked = jnp.concatenate([stacked, stacked], axis=1)
    both = lax.dot_general(
        psi_pair, stacked, (((1,), (1,)), ((), ())), preferred_element_type=jnp.float32
    )
    half = both[:, :m] + both[:, m:]
    vectors = half.shape[0] // m
    half = jnp.concatenate([half[v * m : (v + 1) * m] for v in range(vectors)], axis=1)
    half_hi, half_lo = split(half)
    left_hi, left_lo = split(left)
    left_pair = jnp.concatenate([left_hi, left_lo], axis=1)
    out = jnp.dot(
        left_pair,
        jnp.concatenate([half_hi, half_hi], axis=0),
        preferred_element_type=jnp.float32,
    )
    return out + jnp.dot(left_hi, half_lo, preferred_element_type=jnp.float32)


def prepare(psi, psi_raw, psi_pairs, psi_sem):
    pltpu.make_async_copy(psi, psi_raw, psi_sem).wait()
    sectors, vectors, m, _ = psi_raw.shape

    def one(j, carry):
        hi, lo = split(psi_raw[j].reshape(vectors * m, m))
        psi_pairs[j] = jnp.concatenate([hi, lo], axis=1)
        return carry

    lax.fori_loop(0, sectors, one, 0)


def fetch(left, right, left_buf, right_buf, sems, pair, i, sectors):
    k, j = pair // sectors, pair % sectors
    return (
        pltpu.make_async_copy(left.at[k, j], left_buf.at[i], sems.at[i, 0]),
        pltpu.make_async_copy(right.at[k, j], right_buf.at[i], sems.at[i, 1]),
    )


def collect(codes, base, pairs, low, size, take):
    def one(p, count):
        row = codes[base + p] - low
        hit = (row >= 0) & (row < size)

        @pl.when(hit)
        def _():
            take(count, p, row)

        return count + hit.astype(jnp.int32)

    return lax.fori_loop(0, pairs, one, jnp.int32(0), unroll=4)


def padded(count, group, take, row):
    groups = (count + group - 1) // group

    def one(i, carry):
        take(i, 0, row)
        return carry

    lax.fori_loop(count, groups * group, one, 0)
    return groups


def group_products(g, group, listed, left, right, left_buf, right_buf, sems, psi_pairs, sectors):
    at = [g * group + u for u in range(group)]
    for i in at:
        for copy in fetch(left, right, left_buf, right_buf, sems, listed[i], i, sectors):
            copy.wait()
    return at, [
        apply_pair(left_buf[i], right_buf[i], psi_pairs[listed[i] % sectors]) for i in at
    ]


def sibling_kernel(
    low, size, group, codes, psi, left, right, out,
    listed, left_buf, right_buf, psi_raw, psi_pairs, sems, psi_sem,
):
    terms, sectors, m, _ = left.shape
    vectors = psi.shape[1]
    pltpu.make_async_copy(psi, psi_raw, psi_sem).start()

    def take(i, p, row):
        listed[i] = p
        for copy in fetch(left, right, left_buf, right_buf, sems, p, i, sectors):
            copy.start()

    count = collect(codes, 0, terms * sectors, low, size, take)
    groups = padded(count, group, take, 0)
    prepare(psi, psi_raw, psi_pairs, psi_sem)

    def one(g, carry):
        at, products = group_products(
            g, group, listed, left, right, left_buf, right_buf, sems, psi_pairs, sectors
        )
        for i, product in zip(at, products):
            for v in range(vectors):
                out[i, v] = product[:, v * m : (v + 1) * m]
        return carry

    lax.fori_loop(0, groups, one, 0)


def adder(total, x_count):
    sectors, height = total.shape[2] // VECTORS, total.shape[4]
    x, core = lax.axis_index("ops"), lax.axis_index("sec") % CORES

    def add(code, block):
        row, y_rel = code // PLANES, code % PLANES
        plane, local = row // sectors, row % sectors
        for h in range(x_count):
            x_rel = lax.rem(h - x + x_count, x_count)
            p, q = x_rel, y_rel
            if x_count == PLANES:
                p, q = jnp.where(core == 0, x_rel, y_rel), jnp.where(core == 0, y_rel, x_rel)
            for v in range(VECTORS):
                total[plane, p, v * sectors + local, q] += block(v, h * height)

    return add


def own_kernel(
    low, size, group, x_count, codes, psi, left, right, total,
    listed, rows, left_buf, right_buf, psi_raw, psi_pairs, sems, psi_sem,
):
    terms, sectors, m, _ = left.shape
    height = m // x_count
    pltpu.make_async_copy(psi, psi_raw, psi_sem).start()

    def take(i, p, row):
        listed[i] = p
        rows[i] = row
        for copy in fetch(left, right, left_buf, right_buf, sems, p, i, sectors):
            copy.start()

    count = collect(codes, 0, terms * sectors, low, size, take)
    groups = padded(count, group, take, size)

    def clear(t, carry):
        total[t // x_count, t % x_count] = jnp.zeros(total.shape[2:], jnp.float32)
        return carry

    lax.fori_loop(0, total.shape[0] * x_count, clear, 0)
    prepare(psi, psi_raw, psi_pairs, psi_sem)
    add = adder(total, x_count)

    def one(g, carry):
        at, products = group_products(
            g, group, listed, left, right, left_buf, right_buf, sems, psi_pairs, sectors
        )
        for i, product in zip(at, products):
            add(rows[i], lambda v, h: product[h : h + height, v * m : (v + 1) * m])
        return carry

    lax.fori_loop(0, groups, one, 0)


def merge_kernel(low, size, x_count, pairs, codes, own, *refs):
    del own
    *arrived, total, rows = refs
    height = arrived[0].shape[2] // x_count

    def take(i, p, row):
        rows[i] = row

    count = collect(codes, pairs, pairs, low, size, take)
    add = adder(total, x_count)
    start = 0
    for piece in arrived:

        def merge(i, carry, piece=piece, start=start):
            add(rows[i], lambda v, h: piece[i - start, v, h : h + height])
            return carry

        lax.fori_loop(start, jnp.minimum(count, start + piece.shape[0]), merge, 0)
        start += piece.shape[0]


def group_of(slots):
    return max(d for d in range(1, MOST_IN_GROUP + 1) if slots % d == 0)


def buffers(slots, sectors, vectors, m):
    return [
        pltpu.VMEM((slots, m, m), jnp.float32),
        pltpu.VMEM((slots, m, m), jnp.float32),
        pltpu.VMEM((sectors, vectors, m, m), jnp.float32),
        pltpu.VMEM((sectors, vectors * m, 2 * m), jnp.bfloat16),
        pltpu.SemaphoreType.DMA((slots, 2)),
        pltpu.SemaphoreType.DMA,
    ]


def cost(slots, vectors, m):
    return pl.CostEstimate(
        flops=slots * vectors * 4 * m**3,
        bytes_accessed=slots * (2 + vectors) * m * m * 4,
        transcendentals=0,
    )


def in_hbm(*arrays):
    return [pltpu.with_memory_space_constraint(a, pltpu.HBM) for a in arrays]


def run_sibling(low, size, slots, codes, psi, left, right):
    sectors, m = left.shape[1], left.shape[2]
    vectors = psi.shape[1]
    return pl.pallas_call(
        functools.partial(sibling_kernel, low, size, group_of(slots)),
        out_shape=pltpu.VMEM((slots, vectors, m, m), jnp.float32),
        in_specs=[pl.BlockSpec(memory_space=pltpu.SMEM)] + [pl.BlockSpec(memory_space=pl.ANY)] * 3,
        out_specs=pl.BlockSpec(memory_space=pltpu.VMEM),
        scratch_shapes=[pltpu.SMEM((slots,), jnp.int32), *buffers(slots, sectors, vectors, m)],
        compiler_params=pltpu.CompilerParams(vmem_limit_bytes=24 << 20),
        cost_estimate=cost(slots, vectors, m),
        name="sibling_contributions",
    )(codes, *in_hbm(psi, left, right))


def run_own(low, size, slots, x_count, codes, psi, left, right):
    sectors, m = left.shape[1], left.shape[2]
    vectors = psi.shape[1]
    planes = size // (PLANES * sectors)
    shape = (planes + 1, x_count, vectors * sectors, PLANES, m // x_count, m)
    return pl.pallas_call(
        functools.partial(own_kernel, low, size, group_of(slots), x_count),
        out_shape=pltpu.VMEM(shape, jnp.float32),
        in_specs=[pl.BlockSpec(memory_space=pltpu.SMEM)] + [pl.BlockSpec(memory_space=pl.ANY)] * 3,
        out_specs=pl.BlockSpec(memory_space=pltpu.VMEM),
        scratch_shapes=[pltpu.SMEM((slots,), jnp.int32)] * 2
        + buffers(slots, sectors, vectors, m),
        compiler_params=pltpu.CompilerParams(vmem_limit_bytes=32 << 20),
        cost_estimate=cost(slots, vectors, m),
        name="own_sums",
    )(codes, *in_hbm(psi, left, right))


def run_merge(low, size, slots, x_count, pairs, codes, own, *arrived):
    return pl.pallas_call(
        functools.partial(merge_kernel, low, size, x_count, pairs),
        out_shape=pltpu.VMEM(own.shape, jnp.float32),
        in_specs=[pl.BlockSpec(memory_space=pltpu.SMEM)]
        + [pl.BlockSpec(memory_space=pltpu.VMEM)] * (1 + len(arrived)),
        out_specs=pl.BlockSpec(memory_space=pltpu.VMEM),
        scratch_shapes=[pltpu.SMEM((slots,), jnp.int32)],
        input_output_aliases={1: 0},
        compiler_params=pltpu.CompilerParams(vmem_limit_bytes=32 << 20),
        name="merge_sibling",
    )(codes, own, *arrived)


def shards(wavefunction, left_blocks, right_blocks, target_owner, target_local):
    sec_count = lax.axis_size("sec")
    x_count = lax.axis_size("ops")
    depth = sec_count // (PLANES * CORES)
    terms, sectors, m, _ = left_blocks.shape
    pairs = terms * sectors
    capacity = (pairs + sec_count - 1) // sec_count + 1
    me = lax.axis_index("sec")
    z, y, c = me // (PLANES * CORES), (me // CORES) % PLANES, me % CORES

    chunks = [list(range(depth // 2, 0, -1)), [*range(depth // 2 + 1, depth), 0]]
    order = [r for chunk in chunks for r in chunk]

    def rows_of(table):
        return jnp.concatenate(
            [lax.dynamic_slice_in_dim(table, d, 1, 0) for d in (me, me + 1 - 2 * c)]
        ).reshape(2 * pairs)

    owner = rows_of(target_owner[0, :, :, :, 0].reshape(sec_count, pairs))
    local = rows_of(target_local[0].reshape(sec_count, pairs))
    z_rel = (owner // (CORES * PLANES) - z + depth) % depth
    z_place = sum(jnp.where(z_rel == r, i, 0) for i, r in enumerate(order))
    y_rel = ((owner // CORES) % PLANES - y + PLANES) % PLANES
    c_rel = (owner % CORES - c + CORES) % CORES
    codes = ((c_rel * depth + z_place) * sectors + local) * PLANES + y_rel

    def at(x, z, y, c):
        place = ((z % depth) * PLANES + y % PLANES) * CORES + c % CORES
        return x % x_count * sec_count + place

    everyone = [
        (x, z, y, c)
        for x in range(x_count)
        for z in range(depth)
        for y in range(PLANES)
        for c in range(CORES)
    ]

    def to(target):
        return [(at(*d), at(*target(*d))) for d in everyone]

    swap_core = to(lambda x, z, y, c: (x, z, y, c + 1))
    next_x = to(lambda x, z, y, c: (x + 1, z, y, c))
    next_y = to(lambda x, z, y, c: (x, z, y + 1, c))
    shift = [to(lambda x, z, y, c, r=r: (x, z + r, y, c)) for r in range(depth)]
    first, second = next_x, next_y
    if x_count == PLANES:
        first = to(lambda x, z, y, c: (x + 1, z, y, c) if c == 0 else (x, z, y + 1, c))
        second = to(lambda x, z, y, c: (x, z, y + 1, c) if c == 0 else (x + 1, z, y, c))

    def send(message, perm):
        return lax.ppermute(message, ("ops", "sec"), perm)

    def ring(parts, perm, before=(), done=()):
        moving = after(parts[-1], *before)
        for part in parts[-2::-1]:
            moving = after(send(moving, perm), *done) + part
        return moving

    def fold_first(sums, count, before=(), done=()):
        return ring([sums[p, count] for p in range(x_count)], first, before, done)

    def fold_second(sums, before=()):
        return ring([sums[:, q] for q in range(PLANES)], second, before)

    def after(value, *done):
        return lax.optimization_barrier((value, done))[0] if done else value

    arrays = (wavefunction, left_blocks, right_blocks)
    cut = sectors + sectors // 2
    beside = (1, depth - 1)

    def share(r):
        return slice(0, cut if r == 0 or r in beside else VECTORS * sectors)

    sums, by_rel, halves = [], {}, []
    start = 0
    for rels in chunks:
        span = [PLANES * n for n in (start * sectors, len(rels) * sectors, len(rels) * capacity)]
        sent = run_sibling(
            span[0] + depth * PLANES * sectors, *span[1:], after(codes, *sums), *arrays
        )
        own = run_own(*span, x_count, after(codes, sent), *arrays)
        arrived = [send(part, swap_core) for part in jnp.split(sent, 1 + len(sums))]
        if sums:
            halves = [fold_first(by_rel[order[0]], share(order[0]), done=[own])]
            own = after(own, *halves)
        sums.append(run_merge(*span, x_count, pairs, codes, own, *arrived))
        for i, r in enumerate(rels):
            by_rel[r] = sums[-1][i]
        start += len(rels)

    early = [send(by_rel[r][:, cut:], shift[r]) for r in beside]
    late = []
    for i, r in enumerate(order):
        if i == 1:
            halves.append(fold_first(by_rel[r], share(r), done=[sums[-1], whole]))
        if i > 1:
            halves.append(fold_first(by_rel[r], share(r), before=[halves[i - 2]]))
        whole = fold_second(halves[i])
        late.append(send(whole, shift[r]) if r else whole)
    tail = fold_first(by_rel[0][:, cut:] + sum(early), slice(None), before=[halves[-2]])
    tail = fold_second(tail, before=late[:1])
    total = sum(w[:cut] for w in late)
    tail = tail + sum(w[cut:] for w in late if w.shape[0] > cut)
    return jnp.stack([total[:sectors], jnp.concatenate([total[sectors:], tail])], axis=1)


def solution(mesh):
    placed = (
        P("sec", None, None, None),
        P("ops", "sec", None, None),
        P("ops", "sec", None, None),
        P("ops", None, None, None, None),
        P("ops", None, None, None),
    )
    return jax.shard_map(
        shards, mesh=mesh, in_specs=placed, out_specs=P("sec", None, "ops", None), check_vma=False
    )
```

```python
import functools

import jax
import jax.numpy as jnp
from jax import lax
from jax.experimental import pallas as pl
from jax.experimental.pallas import tpu as pltpu
from jax.sharding import PartitionSpec as P

CORES = 2
PLANES = 2
VECTORS = 2
MOST_IN_GROUP = 10


def split(x):
    hi = x.astype(jnp.bfloat16)
    lo = (x - hi.astype(jnp.float32)).astype(jnp.bfloat16)
    return hi, lo


def apply_pair(left, right, psi_pair):
    m = left.shape[0]
    right_hi, right_lo = split(right)
    stacked = jnp.concatenate([right_hi, right_lo], axis=0)
    stacked = jnp.concatenate([stacked, stacked], axis=1)
    both = lax.dot_general(
        psi_pair, stacked, (((1,), (1,)), ((), ())), preferred_element_type=jnp.float32
    )
    half = both[:, :m] + both[:, m:]
    vectors = half.shape[0] // m
    half = jnp.concatenate([half[v * m : (v + 1) * m] for v in range(vectors)], axis=1)
    half_hi, half_lo = split(half)
    left_hi, left_lo = split(left)
    left_pair = jnp.concatenate([left_hi, left_lo], axis=1)
    out = jnp.dot(
        left_pair,
        jnp.concatenate([half_hi, half_hi], axis=0),
        preferred_element_type=jnp.float32,
    )
    return out + jnp.dot(left_hi, half_lo, preferred_element_type=jnp.float32)


def prepare(psi, psi_raw, psi_pairs, psi_sem):
    pltpu.make_async_copy(psi, psi_raw, psi_sem).wait()
    sectors, vectors, m, _ = psi_raw.shape

    def one(j, carry):
        hi, lo = split(psi_raw[j].reshape(vectors * m, m))
        psi_pairs[j] = jnp.concatenate([hi, lo], axis=1)
        return carry

    lax.fori_loop(0, sectors, one, 0)


def fetch(left, right, left_buf, right_buf, sems, pair, i, sectors):
    k, j = pair // sectors, pair % sectors
    return (
        pltpu.make_async_copy(left.at[k, j], left_buf.at[i], sems.at[i, 0]),
        pltpu.make_async_copy(right.at[k, j], right_buf.at[i], sems.at[i, 1]),
    )


def collect(codes, base, pairs, low, size, take):
    def one(p, count):
        row = codes[base + p] - low
        hit = (row >= 0) & (row < size)

        @pl.when(hit)
        def _():
            take(count, p, row)

        return count + hit.astype(jnp.int32)

    return lax.fori_loop(0, pairs, one, jnp.int32(0), unroll=16)


def row_of(other, pairs):
    return ((lax.axis_index("sec") + other) % CORES) * pairs


def padded(count, group, take, row):
    groups = (count + group - 1) // group

    def one(i, carry):
        take(i, 0, row)
        return carry

    lax.fori_loop(count, groups * group, one, 0)
    return groups


def group_products(g, group, listed, left, right, left_buf, right_buf, sems, psi_pairs, sectors):
    at = [g * group + u for u in range(group)]
    for i in at:
        for copy in fetch(left, right, left_buf, right_buf, sems, listed[i], i, sectors):
            copy.wait()
    return at, [
        apply_pair(left_buf[i], right_buf[i], psi_pairs[listed[i] % sectors]) for i in at
    ]


def sibling_kernel(
    low, size, group, codes, psi, left, right, out,
    listed, left_buf, right_buf, psi_raw, psi_pairs, sems, psi_sem,
):
    terms, sectors, m, _ = left.shape
    vectors = psi.shape[1]
    pltpu.make_async_copy(psi, psi_raw, psi_sem).start()

    def take(i, p, row):
        listed[i] = p
        for copy in fetch(left, right, left_buf, right_buf, sems, p, i, sectors):
            copy.start()

    count = collect(codes, row_of(0, terms * sectors), terms * sectors, low, size, take)
    groups = padded(count, group, take, 0)
    prepare(psi, psi_raw, psi_pairs, psi_sem)

    def one(g, carry):
        at, products = group_products(
            g, group, listed, left, right, left_buf, right_buf, sems, psi_pairs, sectors
        )
        for i, product in zip(at, products):
            for v in range(vectors):
                out[i, v] = product[:, v * m : (v + 1) * m]
        return carry

    lax.fori_loop(0, groups, one, 0)


def adder(total, x_count):
    sectors, height = total.shape[2] // VECTORS, total.shape[4]
    x, core = lax.axis_index("ops"), lax.axis_index("sec") % CORES

    def add(code, block):
        row, y_rel = code // PLANES, code % PLANES
        plane, local = row // sectors, row % sectors
        for h in range(x_count):
            x_rel = lax.rem(h - x + x_count, x_count)
            p, q = x_rel, y_rel
            if x_count == PLANES:
                p, q = jnp.where(core == 0, x_rel, y_rel), jnp.where(core == 0, y_rel, x_rel)
            for v in range(VECTORS):
                total[plane, p, v * sectors + local, q] += block(v, h * height)

    return add


def own_kernel(
    low, size, group, x_count, codes, psi, left, right, total,
    listed, rows, left_buf, right_buf, psi_raw, psi_pairs, sems, psi_sem,
):
    terms, sectors, m, _ = left.shape
    height = m // x_count
    pltpu.make_async_copy(psi, psi_raw, psi_sem).start()

    def take(i, p, row):
        listed[i] = p
        rows[i] = row
        for copy in fetch(left, right, left_buf, right_buf, sems, p, i, sectors):
            copy.start()

    count = collect(codes, row_of(0, terms * sectors), terms * sectors, low, size, take)
    groups = padded(count, group, take, size)

    def clear(t, carry):
        total[t // x_count, t % x_count] = jnp.zeros(total.shape[2:], jnp.float32)
        return carry

    lax.fori_loop(0, total.shape[0] * x_count, clear, 0)
    prepare(psi, psi_raw, psi_pairs, psi_sem)
    add = adder(total, x_count)

    def one(g, carry):
        at, products = group_products(
            g, group, listed, left, right, left_buf, right_buf, sems, psi_pairs, sectors
        )
        for i, product in zip(at, products):
            add(rows[i], lambda v, h: product[h : h + height, v * m : (v + 1) * m])
        return carry

    lax.fori_loop(0, groups, one, 0)


def merge_kernel(low, size, x_count, pairs, codes, own, *refs):
    del own
    *arrived, total, rows = refs
    height = arrived[0].shape[2] // x_count

    def take(i, p, row):
        rows[i] = row

    count = collect(codes, row_of(1, pairs), pairs, low, size, take)
    add = adder(total, x_count)
    start = 0
    for piece in arrived:

        def merge(i, carry, piece=piece, start=start):
            add(rows[i], lambda v, h: piece[i - start, v, h : h + height])
            return carry

        lax.fori_loop(start, jnp.minimum(count, start + piece.shape[0]), merge, 0)
        start += piece.shape[0]


def group_of(slots):
    return max(d for d in range(1, MOST_IN_GROUP + 1) if slots % d == 0)


def buffers(slots, sectors, vectors, m):
    return [
        pltpu.VMEM((slots, m, m), jnp.float32),
        pltpu.VMEM((slots, m, m), jnp.float32),
        pltpu.VMEM((sectors, vectors, m, m), jnp.float32),
        pltpu.VMEM((sectors, vectors * m, 2 * m), jnp.bfloat16),
        pltpu.SemaphoreType.DMA((slots, 2)),
        pltpu.SemaphoreType.DMA,
    ]


def cost(slots, vectors, m):
    return pl.CostEstimate(
        flops=slots * vectors * 4 * m**3,
        bytes_accessed=slots * (2 + vectors) * m * m * 4,
        transcendentals=0,
    )


def in_hbm(*arrays):
    return [pltpu.with_memory_space_constraint(a, pltpu.HBM) for a in arrays]


def run_sibling(low, size, slots, codes, psi, left, right):
    sectors, m = left.shape[1], left.shape[2]
    vectors = psi.shape[1]
    return pl.pallas_call(
        functools.partial(sibling_kernel, low, size, group_of(slots)),
        out_shape=pltpu.VMEM((slots, vectors, m, m), jnp.float32),
        in_specs=[pl.BlockSpec(memory_space=pltpu.SMEM)] + [pl.BlockSpec(memory_space=pl.ANY)] * 3,
        out_specs=pl.BlockSpec(memory_space=pltpu.VMEM),
        scratch_shapes=[pltpu.SMEM((slots,), jnp.int32), *buffers(slots, sectors, vectors, m)],
        compiler_params=pltpu.CompilerParams(vmem_limit_bytes=24 << 20),
        cost_estimate=cost(slots, vectors, m),
        name="sibling_contributions",
    )(codes, *in_hbm(psi, left, right))


def run_own(low, size, slots, x_count, codes, psi, left, right):
    sectors, m = left.shape[1], left.shape[2]
    vectors = psi.shape[1]
    planes = size // (PLANES * sectors)
    shape = (planes + 1, x_count, vectors * sectors, PLANES, m // x_count, m)
    return pl.pallas_call(
        functools.partial(own_kernel, low, size, group_of(slots), x_count),
        out_shape=pltpu.VMEM(shape, jnp.float32),
        in_specs=[pl.BlockSpec(memory_space=pltpu.SMEM)] + [pl.BlockSpec(memory_space=pl.ANY)] * 3,
        out_specs=pl.BlockSpec(memory_space=pltpu.VMEM),
        scratch_shapes=[pltpu.SMEM((slots,), jnp.int32)] * 2
        + buffers(slots, sectors, vectors, m),
        compiler_params=pltpu.CompilerParams(vmem_limit_bytes=32 << 20),
        cost_estimate=cost(slots, vectors, m),
        name="own_sums",
    )(codes, *in_hbm(psi, left, right))


def run_merge(low, size, slots, x_count, pairs, codes, own, *arrived):
    return pl.pallas_call(
        functools.partial(merge_kernel, low, size, x_count, pairs),
        out_shape=pltpu.VMEM(own.shape, jnp.float32),
        in_specs=[pl.BlockSpec(memory_space=pltpu.SMEM)]
        + [pl.BlockSpec(memory_space=pltpu.VMEM)] * (1 + len(arrived)),
        out_specs=pl.BlockSpec(memory_space=pltpu.VMEM),
        scratch_shapes=[pltpu.SMEM((slots,), jnp.int32)],
        input_output_aliases={1: 0},
        compiler_params=pltpu.CompilerParams(vmem_limit_bytes=32 << 20),
        name="merge_sibling",
    )(codes, own, *arrived)


def shards(wavefunction, left_blocks, right_blocks, target_owner, target_local):
    sec_count = lax.axis_size("sec")
    x_count = lax.axis_size("ops")
    depth = sec_count // (PLANES * CORES)
    terms, sectors, m, _ = left_blocks.shape
    pairs = terms * sectors
    capacity = (pairs + sec_count - 1) // sec_count + 1
    me = lax.axis_index("sec")
    z, y, c = me // (PLANES * CORES), (me // CORES) % PLANES, me % CORES

    chunks = [list(range(depth // 2, 0, -1)), [*range(depth // 2 + 1, depth), 0]]
    order = [r for chunk in chunks for r in chunk]

    def of_chip(table):
        return lax.dynamic_slice_in_dim(table, me - c, CORES, 0).reshape(CORES * pairs)

    owner = of_chip(target_owner.reshape(sec_count, pairs))
    local = of_chip(target_local.reshape(sec_count, pairs))
    z_rel = (owner // (CORES * PLANES) - z + depth) % depth
    z_place = sum(jnp.where(z_rel == r, i, 0) for i, r in enumerate(order))
    y_rel = ((owner // CORES) % PLANES - y + PLANES) % PLANES
    c_rel = (owner % CORES - c + CORES) % CORES
    codes = ((c_rel * depth + z_place) * sectors + local) * PLANES + y_rel

    def at(x, z, y, c):
        place = ((z % depth) * PLANES + y % PLANES) * CORES + c % CORES
        return x % x_count * sec_count + place

    everyone = [
        (x, z, y, c)
        for x in range(x_count)
        for z in range(depth)
        for y in range(PLANES)
        for c in range(CORES)
    ]

    def to(target):
        return [(at(*d), at(*target(*d))) for d in everyone]

    swap_core = to(lambda x, z, y, c: (x, z, y, c + 1))
    next_x = to(lambda x, z, y, c: (x + 1, z, y, c))
    next_y = to(lambda x, z, y, c: (x, z, y + 1, c))
    shift = [to(lambda x, z, y, c, r=r: (x, z + r, y, c)) for r in range(depth)]
    first, second = next_x, next_y
    if x_count == PLANES:
        first = to(lambda x, z, y, c: (x + 1, z, y, c) if c == 0 else (x, z, y + 1, c))
        second = to(lambda x, z, y, c: (x, z, y + 1, c) if c == 0 else (x + 1, z, y, c))

    def send(message, perm):
        return lax.ppermute(message, ("ops", "sec"), perm)

    def ring(parts, perm, before=(), done=()):
        moving = after(parts[-1], *before)
        for part in parts[-2::-1]:
            moving = after(send(moving, perm), *done) + part
        return moving

    def fold_first(sums, count, before=(), done=()):
        return ring([sums[p, count] for p in range(x_count)], first, before, done)

    def fold_second(sums, before=()):
        return ring([sums[:, q] for q in range(PLANES)], second, before)

    def after(value, *done):
        return lax.optimization_barrier((value, done))[0] if done else value

    arrays = (wavefunction, left_blocks, right_blocks)
    cut = sectors + sectors // 2
    beside = (1, depth - 1)

    def share(r):
        return slice(0, cut if r == 0 or r in beside else VECTORS * sectors)

    sums, by_rel, halves = [], {}, []
    start = 0
    for rels in chunks:
        span = [PLANES * n for n in (start * sectors, len(rels) * sectors, len(rels) * capacity)]
        sent = run_sibling(
            span[0] + depth * PLANES * sectors, *span[1:], after(codes, *sums), *arrays
        )
        own = run_own(*span, x_count, after(codes, sent), *arrays)
        arrived = [send(part, swap_core) for part in jnp.split(sent, 1 + len(sums))]
        if sums:
            halves = [fold_first(by_rel[order[0]], share(order[0]), done=[own])]
            own = after(own, *halves)
        sums.append(run_merge(*span, x_count, pairs, codes, own, *arrived))
        for i, r in enumerate(rels):
            by_rel[r] = sums[-1][i]
        start += len(rels)

    early = [send(by_rel[r][:, cut:], shift[r]) for r in beside]
    late = []
    for i, r in enumerate(order):
        if i == 1:
            halves.append(fold_first(by_rel[r], share(r), done=[sums[-1], whole]))
        if i > 1:
            halves.append(fold_first(by_rel[r], share(r), before=[halves[i - 2]]))
        whole = fold_second(halves[i])
        late.append(send(whole, shift[r]) if r else whole)
    tail = fold_first(by_rel[0][:, cut:] + sum(early), slice(None), before=[halves[-2]])
    tail = fold_second(tail, before=late[:1])
    total = sum(w[:cut] for w in late)
    tail = tail + sum(w[cut:] for w in late if w.shape[0] > cut)
    return jnp.stack([total[:sectors], jnp.concatenate([total[sectors:], tail])], axis=1)


def solution(mesh):
    placed = (
        P("sec", None, None, None),
        P("ops", "sec", None, None),
        P("ops", "sec", None, None),
        P("ops", None, None, None, None),
        P("ops", None, None, None),
    )
    return jax.shard_map(
        shards, mesh=mesh, in_specs=placed, out_specs=P("sec", None, "ops", None), check_vma=False
    )
```
